128 devices in a mesh: row: 8 (over x, y_lo), col: 16 (over z, y_hi, core).
Axes of the slice: x: 4, y: 4 (y_hi: 2, y_lo: 2; y = y_hi * 2 + y_lo), z: 4, core: 2. Of those that a mesh axis runs over, the one named last changes fastest.
Arguments:
- dense_in: bfloat16 [1024, 28672], P('col', 'row'), may hold values from -6 to 6
- pruned_in: bfloat16 [1024, 28672], P('col', 'row'), may hold values from -6 to 6
- weight: bfloat16 [28672, 8192], P('row', 'col'), may hold values from -0.03125 to 0.03125
- keep_bits: int32 [512, 28672], P('col', 'row'), may hold values from 0 to 65535
Outputs:
- gram_tile: float32 [8192, 8192], P('row', 'col')
- cross_tile: float32 [8192, 8192], P('row', 'col')
The draws below stay inside these ranges and needn't reach their ends.
Inputs may be any that keep to these rules, and one draw needn't show every extreme that they name: `keep_bits`: each word holds 16 independent flags, each 1 with probability one half.
All inputs are finite; a program needn't handle non-finite values.
Results may differ from the reference program's by a relative error of at most 0.0039.
Values may be sent and summed in bfloat16 or wider, within the bound.
No kernel may reach another device: no remote copies, remote signals or barrier semaphores. Data moves between devices by JAX's collectives and lax.ppermute only.
A program may use at most 128 MiB of HBM per device.

```python
import jax
import jax.numpy as jnp
from jax import lax

D = 8192
FF = 28672
TOKENS = 1024
WORDS = 512
N_COL = 16


def place_ends(result, rng, low, top_value):
    extent = result.shape
    index_at = [jax.random.randint(jax.random.fold_in(rng, axis), (), 0, extent[axis]) for axis in range(len(extent))]
    result = result.at[tuple(index_at)].set(low)
    longest = extent.index(max(extent))
    index_at[longest] = (index_at[longest] + 1) % extent[longest]
    return result.at[tuple(index_at)].set(top_value)


def steps_of(own_key, extent, shards, low, largest):
    level = 1.0
    for axis_at, parts in shards:
        draws = jax.random.uniform(jax.random.fold_in(jax.random.fold_in(own_key, 6), axis_at), (parts,), jnp.float32, low / len(shards), largest / len(shards))
        level = level * jnp.repeat(jnp.exp(draws), extent[axis_at] // parts).reshape((-1,) + (1,) * (len(extent) - 1 - axis_at))
    return level


def gaussian(stream_key, shape, spread, reach, shards=(), kind=jnp.bfloat16):
    factor_of = steps_of(stream_key, shape, shards, -0.22, 0.18) if shards else 1.0
    array = jax.random.normal(stream_key, shape, jnp.float32) * spread * factor_of
    return jnp.minimum(jnp.maximum(array, -reach), reach).astype(kind)


def setup_inputs(seed: int = 0) -> dict:
    arg_keys = jax.random.split(jax.random.key(seed), 5)
    dense_in = gaussian(arg_keys[0], (TOKENS, FF), 1.0, 6.0, ((0, 16), (1, 8)))
    pruned_in = gaussian(arg_keys[1], (TOKENS, FF), 1.0, 6.0, ((0, 16), (1, 8)))
    weight = gaussian(arg_keys[2], (FF, D), FF ** -0.5, 0.03125, ((0, 8), (1, 16)))
    keep_bits = place_ends(jax.random.randint(arg_keys[3], (WORDS, FF), 0, 65536), jax.random.fold_in(arg_keys[3], 1), 0, 65535).astype(jnp.int32)
    return {"dense_in": dense_in, "pruned_in": pruned_in, "weight": weight, "keep_bits": keep_bits}


def unpack_block(word_block, columns):
    shifts = jnp.arange(16, dtype=jnp.int32)
    flag_bits = jnp.right_shift(word_block[:, None, :], shifts[None, :, None]) & 1
    return flag_bits.reshape(word_block.shape[0] * 16, word_block.shape[1])[:columns]


def reference(dense_in, pruned_in, weight, keep_bits):
    columns = D // N_COL
    per_block = keep_bits.shape[0] // N_COL
    keep_flags = jnp.concatenate([unpack_block(keep_bits[index * per_block:(index + 1) * per_block], columns) for index in range(N_COL)], 0)
    pruned_w = jnp.where(keep_flags.T == 1, weight, jnp.zeros_like(weight))
    dense_out = jnp.dot(dense_in, weight, preferred_element_type=jnp.float32)
    pruned_out = jnp.dot(pruned_in, pruned_w, preferred_element_type=jnp.float32)
    pruned_b = pruned_out.astype(jnp.bfloat16)
    difference = (dense_out - pruned_out).astype(jnp.bfloat16)
    dims = (((0,), (0,)), ((), ()))
    gram_tile = lax.dot_general(pruned_b, pruned_b, dims, preferred_element_type=jnp.float32) / TOKENS
    cross_tile = lax.dot_general(difference, pruned_b, dims, preferred_element_type=jnp.float32) / TOKENS
    return gram_tile, cross_tile
```

```python
import jax
import jax.numpy as jnp
from jax import lax
from jax.sharding import Mesh
from jax.sharding import PartitionSpec as P

ROW = ("x", "yl")
SIDE = ("z", "yh")
COL = ("z", "yh", "k")
BF = jnp.bfloat16
F32 = jnp.float32


def step(a, dz, dy):
    nz, ny = lax.axis_size("z"), lax.axis_size("yh")
    pairs = [
        (z * ny + y, ((z + dz) % nz) * ny + (y + dy) % ny) for z in range(nz) for y in range(ny)
    ]
    return lax.ppermute(a, SIDE, pairs)


def swap(a):
    return lax.ppermute(a, "k", [(0, 1), (1, 0)])


def gathered(own):
    half = own.shape[0] // 2
    up, down = step(own, 1, 0), step(own, 3, 0)
    side = step(own, 0, 1)
    far = jnp.concatenate([step(up[:half], 1, 0), step(down[half:], 3, 0)], 0)
    side_up, side_down = step(side, 1, 0), step(side, 3, 0)
    side_far = step(far, 0, 1)
    return [own, side, down, side_down, far, side_far, up, side_up]


def transposed(a):
    pairs = []
    for r in range(8):
        for c in range(8):
            for k in range(2):
                pairs.append(((r * 8 + c) * 2 + k, (c * 8 + r) * 2 + k))
    return lax.ppermute(a, ROW + COL, pairs)


def spread(a, axes):
    n = lax.axis_size(axes)
    return lax.all_to_all(jnp.broadcast_to(a, (n,) + a.shape), axes, 0, 0, tiled=True)


def keep_mask(words):
    shifts = jnp.arange(16, dtype=jnp.int32)
    bits = jnp.right_shift(words[:, None, :], shifts[None, :, None]) & 1
    return bits.reshape(words.shape[0] * 16, words.shape[1]).T == 1


def dots(blocks, mine, other):
    out = []
    for part in (blocks[:4], blocks[4:]):
        a = jnp.concatenate(part, 0)
        halves = [jnp.dot(a, w, preferred_element_type=F32) for w in (mine, other)]
        out.append(jnp.concatenate(halves, 1))
    return jnp.concatenate(out, 0).reshape(8, -1, 2 * mine.shape[1])


def summed(partial):
    z, yh = lax.axis_index("z"), lax.axis_index("yh")
    me = lax.axis_index(ROW)
    order = [((place // 2 - z) % 4) * 2 + (place % 2 - yh) % 2 for place in range(8)]
    sent = jnp.stack([lax.dynamic_index_in_dim(partial, i, 0, False).astype(BF) for i in order])
    at_me = ((me // 2 - z) % 4) * 2 + (me % 2 - yh) % 2
    own = lax.dynamic_index_in_dim(partial, at_me, 0, False)
    came = lax.all_to_all(sent, ROW, 0, 0, tiled=True)
    rest = own - own.astype(BF).astype(F32)
    total = jnp.sum(came.astype(F32), 0) + rest
    half = total.shape[1] // 2
    swapped = jnp.concatenate([total[:, half:], total[:, :half]], 1)
    return jnp.where(lax.axis_index("k") == 0, total, swapped).astype(BF)


def both(own):
    return jnp.concatenate([own, swap(own)], 0)


def columns(p):
    every = spread(p, ROW).reshape(-1, p.shape[1])
    k = lax.axis_index("k")
    half = p.shape[1] // 2
    mine = lax.dynamic_slice_in_dim(every, k * half, half, 1)
    others = lax.dynamic_slice_in_dim(every, (1 - k) * half, half, 1)
    return jnp.concatenate([mine, swap(others)], 0)


def rows(s):
    every = spread(transposed(s), SIDE)
    return both(every.reshape(-1, s.shape[1]))


def local(dense_in, pruned_in, weight, keep_bits):
    tokens = dense_in.shape[0] * lax.axis_size(COL)
    pruned_blocks = gathered(pruned_in)
    pruned_w = jnp.where(keep_mask(keep_bits), weight, jnp.zeros_like(weight))
    pruned_part = dots(pruned_blocks, pruned_w, swap(pruned_w))
    dense_blocks = gathered(dense_in)
    dense_part = dots(dense_blocks, weight, swap(weight))
    p = summed(pruned_part)
    cols = columns(p)
    rows_p = rows(p)
    d = summed(dense_part - pruned_part)
    rows_d = rows(d)
    dims = (((0,), (0,)), ((), ()))
    gram_tile = lax.dot_general(rows_p, cols, dims, preferred_element_type=F32) / tokens
    cross_tile = lax.dot_general(rows_d, cols, dims, preferred_element_type=F32) / tokens
    return (gram_tile, cross_tile)


def solution(mesh):
    split = Mesh(mesh.devices.reshape(4, 2, 4, 2, 2), ROW + COL)
    in_specs = (P(COL, ROW), P(COL, ROW), P(ROW, COL), P(COL, ROW))
    out_specs = (P(ROW, COL), P(ROW, COL))
    return jax.shard_map(local, mesh=split, in_specs=in_specs, out_specs=out_specs, check_vma=False)
```

```python
import functools

import jax
import jax.numpy as jnp
from jax import lax
from jax.experimental import pallas as pl
from jax.experimental.pallas import tpu as pltpu
from jax.sharding import Mesh
from jax.sharding import PartitionSpec as P

ROW = ("x", "yl")
SIDE = ("z", "yh")
COL = ("z", "yh", "k")
BF = jnp.bfloat16
F32 = jnp.float32


PLACES = ((0, 0), (0, 1), (3, 0), (1, 0), (3, 1), (1, 1), (2, 0), (2, 1))


def step(a, dz, dy, axes=SIDE):
    nz, ny = lax.axis_size(axes[0]), lax.axis_size(axes[1])
    pairs = [
        (z * ny + y, ((z + dz) % nz) * ny + (y + dy) % ny) for z in range(nz) for y in range(ny)
    ]
    return lax.ppermute(a, axes, pairs)


def swap(a):
    return lax.ppermute(a, "k", [(0, 1), (1, 0)])


def after(a, *done):
    return lax.optimization_barrier((a,) + done)[0]


def transposed(a):
    pairs = []
    for r in range(8):
        for c in range(8):
            for k in range(2):
                pairs.append(((r * 8 + c) * 2 + k, (c * 8 + r) * 2 + k))
    return lax.ppermute(a, ROW + COL, pairs)


def spread(a, axes):
    n = lax.axis_size(axes)
    return lax.all_to_all(jnp.broadcast_to(a, (n,) + a.shape), axes, 0, 0, tiled=True)


def pruned(weight, words):
    n = weight.shape[1]
    rows = words.shape[0]
    halves = jnp.concatenate([words & 255, jnp.right_shift(words, 8)], 0).astype(BF)
    column = jnp.arange(n)
    source = column // 16 + rows * (column % 16 // 8)
    ones = (jnp.arange(2 * rows)[:, None] == source[None, :]).astype(BF)
    dims = (((0,), (0,)), ((), ()))
    byte = lax.dot_general(halves, ones, dims, preferred_element_type=F32).astype(jnp.int32)
    flag = jnp.right_shift(byte, (column % 8)[None, :]) & 1
    return jnp.where(flag == 1, weight, jnp.zeros_like(weight))


def dots(blocks, weights):
    a = jnp.concatenate(blocks, 0)
    outs = [jnp.dot(a, w, preferred_element_type=F32) for w in weights]
    return [o.reshape(len(blocks), -1, o.shape[1]) for o in outs]


def joined(first, second):
    return jnp.concatenate([jnp.concatenate(h, 2) for h in (first, second)], 0)


def place_kernel(at_ref, blocks, out):
    for i in range(8):
        out[at_ref[i]] = blocks[i]


def placed(blocks, at):
    vmem = pl.BlockSpec(memory_space=pltpu.VMEM)
    return pl.pallas_call(
        place_kernel,
        in_specs=[pl.BlockSpec(memory_space=pltpu.SMEM), vmem],
        out_specs=vmem,
        out_shape=jax.ShapeDtypeStruct(blocks.shape, BF),
        compiler_params=pltpu.CompilerParams(vmem_limit_bytes=4 * 1024 * 1024),
        name="placed",
    )(jnp.stack(at).astype(jnp.int32), blocks)


def summed(sent, partial):
    own = lax.dynamic_index_in_dim(partial, lax.axis_index(ROW), 0, False)
    came = lax.all_to_all(sent, ROW, 0, 0, tiled=True)
    total = jnp.sum(came.astype(F32), 0) + (own - own.astype(BF).astype(F32))
    half = total.shape[1] // 2
    crossed = jnp.concatenate([total[:, half:], total[:, :half]], 1)
    return jnp.where(lax.axis_index("k") == 0, total, crossed).astype(BF)


def lookup(table, at):
    out = 0
    for i, t in enumerate(table):
        out = out + jnp.where(at == i, t, 0)
    return out


def columns(blocks):
    x, yl, z, yh = (lax.axis_index(a) for a in ROW + SIDE)
    number = [PLACES.index((i // 2, i % 2)) for i in range(8)]
    at = []
    for a, b in PLACES:
        at.append(lookup(number, (z - x + a + 4) % 4 * 2 + (yh - yl + b + 2) % 2))
    every = placed(blocks, at)
    k = lax.axis_index("k")
    half = every.shape[2] // 2
    mine = lax.dynamic_slice_in_dim(every, k * half, half, 2)
    others = lax.dynamic_slice_in_dim(every, (1 - k) * half, half, 2)
    return mine, swap(others)


def product(rows, cols):
    dims = (((0, 1), (0, 1)), ((), ()))
    return lax.dot_general(rows, cols, dims, preferred_element_type=F32)


def local(dense_in, pruned_in, weight, keep_bits):
    tokens = dense_in.shape[0] * lax.axis_size(COL)
    n = dense_in.shape[0]
    h = n // 2
    p_side, p_up, p_down = step(pruned_in, 0, 1), step(pruned_in, 1, 0), step(pruned_in, 3, 0)
    weight_o = swap(weight)
    pruned_w = pruned(weight, keep_bits)
    p_side, p_up, p_down, pruned_w = lax.optimization_barrier((p_side, p_up, p_down, pruned_w))
    pruned_o = swap(pruned_w)
    p_up2 = step(jnp.concatenate([p_side, p_up[: n // 2]], 0), 1, 0)
    p_down2 = step(jnp.concatenate([p_side, p_down[n // 2 :]], 0), 3, 0)
    d_side = step(after(dense_in, p_side), 0, 1)
    p_up2, p_down2, d_side = lax.optimization_barrier((p_up2, p_down2, d_side))
    p_across = jnp.concatenate([p_up2[n:], p_down2[n:]], 0)
    p_side_across = step(p_across, 0, 1)
    d_pair = jnp.concatenate([dense_in, d_side], 0)
    d_up, d_down = step(d_pair, 1, 0), step(d_pair, 3, 0)
    pruned_ws, dense_ws = (pruned_w, pruned_o), (weight, weight_o)
    p_first = dots([pruned_in, p_side, p_up, p_down], pruned_ws)
    p_second = dots([p_up2[:n], p_down2[:n], p_across, p_side_across], pruned_ws)
    part_p = joined(p_first, p_second)
    sent_p = part_p.astype(BF)
    d_up, d_down, part_p, sent_p = lax.optimization_barrier((d_up, d_down, part_p, sent_p))
    p = summed(sent_p, part_p)
    d_across, d_side_across = step(d_up[:n], 1, 0), step(d_down[n:], 3, 0)
    d_first = dots([dense_in, d_side, d_up[:n], d_down[:n]], dense_ws)
    d_across, d_side_across, p, *d_first = lax.optimization_barrier((d_across, d_side_across, p, *d_first))
    d_second = dots([d_up[n:], d_down[n:], d_across, d_side_across], dense_ws)
    part_d = joined(d_first, d_second) - part_p
    sent_d = part_d.astype(BF)
    p, part_d, sent_d = lax.optimization_barrier((p, part_d, sent_d))
    d = summed(sent_d, part_d)
    t_p = transposed(p)
    d, p, t_p = lax.optimization_barrier((d, p, t_p))
    t_d = transposed(d)
    every = spread(p, ROW)
    t_d, every = lax.optimization_barrier((t_d, every))
    rows = spread(jnp.concatenate([t_p, t_d], 0), SIDE)
    cols = columns(every)
    others = swap(rows)
    gram_tile = (product(rows[:, :n], cols[0]) + product(others[:, :n], cols[1])) / tokens
    cross_tile = (product(rows[:, n:], cols[0]) + product(others[:, n:], cols[1])) / tokens
    return (gram_tile, cross_tile)


def solution(mesh):
    split = Mesh(mesh.devices.reshape(4, 2, 4, 2, 2), ROW + COL)
    in_specs = (P(COL, ROW), P(COL, ROW), P(ROW, COL), P(COL, ROW))
    out_specs = (P(ROW, COL), P(ROW, COL))
    return jax.shard_map(local, mesh=split, in_specs=in_specs, out_specs=out_specs, check_vma=False)
```

```python
import functools

import jax
import jax.numpy as jnp
from jax import lax
from jax.experimental import pallas as pl
from jax.experimental.pallas import tpu as pltpu
from jax.sharding import Mesh
from jax.sharding import PartitionSpec as P

ROW = ("x", "yl")
SIDE = ("z", "yh")
COL = ("z", "yh", "k")
BF = jnp.bfloat16
F32 = jnp.float32


PLACES = ((0, 0), (0, 1), (3, 0), (1, 0), (3, 1), (1, 1), (2, 0), (2, 1))


def step(a, dz, dy, axes=SIDE):
    nz, ny = lax.axis_size(axes[0]), lax.axis_size(axes[1])
    pairs = [
        (z * ny + y, ((z + dz) % nz) * ny + (y + dy) % ny) for z in range(nz) for y in range(ny)
    ]
    return lax.ppermute(a, axes, pairs)


def swap(a):
    return lax.ppermute(a, "k", [(0, 1), (1, 0)])


def after(a, *done):
    return lax.optimization_barrier((a,) + done)[0]


def transposed(a):
    pairs = []
    for r in range(8):
        for c in range(8):
            for k in range(2):
                pairs.append(((r * 8 + c) * 2 + k, (c * 8 + r) * 2 + k))
    return lax.ppermute(a, ROW + COL, pairs)


def spread(a, axes):
    n = lax.axis_size(axes)
    return lax.all_to_all(jnp.broadcast_to(a, (n,) + a.shape), axes, 0, 0, tiled=True)


def pruned(weight, words):
    n = weight.shape[1]
    rows = words.shape[0]
    halves = jnp.concatenate([words & 255, jnp.right_shift(words, 8)], 0).astype(BF)
    column = jnp.arange(n)
    source = column // 16 + rows * (column % 16 // 8)
    ones = (jnp.arange(2 * rows)[:, None] == source[None, :]).astype(BF)
    dims = (((0,), (0,)), ((), ()))
    byte = lax.dot_general(halves, ones, dims, preferred_element_type=F32).astype(jnp.int32)
    flag = jnp.right_shift(byte, (column % 8)[None, :]) & 1
    return jnp.where(flag == 1, weight, jnp.zeros_like(weight))


def dots(blocks, weights):
    a = jnp.concatenate(blocks, 0)
    outs = [jnp.dot(a, w, preferred_element_type=F32) for w in weights]
    return [o.reshape(len(blocks), -1, o.shape[1]) for o in outs]


def joined(first, second):
    return jnp.concatenate([jnp.concatenate(h, 2) for h in (first, second)], 0)


def arrange_kernel(at_ref, pair, up, down, across, side_across, out):
    n = across.shape[0]
    blocks = [pair[:n], pair[n:], up[:n], down[:n], up[n:], down[n:], across[...], side_across[...]]
    for i, b in enumerate(blocks):
        out[at_ref[i]] = b


def arranged(parts, at):
    vmem = pl.BlockSpec(memory_space=pltpu.VMEM)
    return pl.pallas_call(
        arrange_kernel,
        in_specs=[pl.BlockSpec(memory_space=pltpu.SMEM)] + [vmem] * 5,
        out_specs=vmem,
        out_shape=jax.ShapeDtypeStruct((8,) + parts[3].shape, BF),
        compiler_params=pltpu.CompilerParams(vmem_limit_bytes=4 * 1024 * 1024),
        name="arranged",
    )(jnp.stack(at).astype(jnp.int32), *parts)


def start_around(a, axes):
    return jnp.concatenate([a, step(a, 0, 1, axes)], 0)


def ends_around(pair, axes):
    return step(pair, 1, 0, axes), step(pair, 3, 0, axes)


def finish_around(pair, up, down, axes):
    n = pair.shape[0] // 2
    return pair, up, down, step(up[:n], 1, 0, axes), step(down[n:], 3, 0, axes)


def summed(sent, partial):
    own = lax.dynamic_index_in_dim(partial, lax.axis_index(ROW), 0, False)
    came = lax.all_to_all(sent, ROW, 0, 0, tiled=True)
    total = jnp.sum(came.astype(F32), 0) + (own - own.astype(BF).astype(F32))
    half = total.shape[1] // 2
    crossed = jnp.concatenate([total[:, half:], total[:, :half]], 1)
    return jnp.where(lax.axis_index("k") == 0, total, crossed).astype(BF)


def lookup(table, at):
    out = 0
    for i, t in enumerate(table):
        out = out + jnp.where(at == i, t, 0)
    return out


def columns(parts):
    x, yl, z, yh = (lax.axis_index(a) for a in ROW + SIDE)
    number = [PLACES.index((i // 2, i % 2)) for i in range(8)]
    at = []
    for a, b in PLACES:
        member = (x + a) % 4 * 2 + (yl + b) % 2
        far = [lookup([place[q] for place in PLACES], member) for q in range(2)]
        at.append(lookup(number, (z - x + far[0] + 4) % 4 * 2 + (yh - yl + far[1] + 2) % 2))
    every = arranged(parts, at)
    k = lax.axis_index("k")
    half = every.shape[2] // 2
    mine = lax.dynamic_slice_in_dim(every, k * half, half, 2)
    others = lax.dynamic_slice_in_dim(every, (1 - k) * half, half, 2)
    return mine, swap(others)


def product(rows, cols):
    dims = (((0, 1), (0, 1)), ((), ()))
    return lax.dot_general(rows, cols, dims, preferred_element_type=F32)


def local(dense_in, pruned_in, weight, keep_bits):
    tokens = dense_in.shape[0] * lax.axis_size(COL)
    n = dense_in.shape[0]
    h = n // 2
    p_side, p_up, p_down = step(pruned_in, 0, 1), step(pruned_in, 1, 0), step(pruned_in, 3, 0)
    weight_o = swap(weight)
    pruned_w = pruned(weight, keep_bits)
    p_side, p_up, p_down, pruned_w = lax.optimization_barrier((p_side, p_up, p_down, pruned_w))
    pruned_o = swap(pruned_w)
    p_up2 = step(jnp.concatenate([p_side, p_up[: n // 2]], 0), 1, 0)
    p_down2 = step(jnp.concatenate([p_side, p_down[n // 2 :]], 0), 3, 0)
    d_side = step(after(dense_in, p_side), 0, 1)
    p_up2, p_down2, d_side = lax.optimization_barrier((p_up2, p_down2, d_side))
    p_across = jnp.concatenate([p_up2[n:], p_down2[n:]], 0)
    p_side_across = step(p_across, 0, 1)
    d_pair = jnp.concatenate([dense_in, d_side], 0)
    d_up, d_down = step(d_pair, 1, 0), step(d_pair, 3, 0)
    pruned_ws, dense_ws = (pruned_w, pruned_o), (weight, weight_o)
    p_first = dots([pruned_in, p_side, p_up, p_down], pruned_ws)
    p_second = dots([p_up2[:n], p_down2[:n], p_across, p_side_across], pruned_ws)
    part_p = joined(p_first, p_second)
    sent_p = part_p.astype(BF)
    d_up, d_down, part_p, sent_p = lax.optimization_barrier((d_up, d_down, part_p, sent_p))
    p = summed(sent_p, part_p)
    d_across, d_side_across = step(d_up[:n], 1, 0), step(d_down[n:], 3, 0)
    d_first = dots([dense_in, d_side, d_up[:n], d_down[:n]], dense_ws)
    d_across, d_side_across, p, *d_first = lax.optimization_barrier((d_across, d_side_across, p, *d_first))
    d_second = dots([d_up[n:], d_down[n:], d_across, d_side_across], dense_ws)
    part_d = joined(d_first, d_second) - part_p
    sent_d = part_d.astype(BF)
    p, part_d, sent_d = lax.optimization_barrier((p, part_d, sent_d))
    d = summed(sent_d, part_d)
    t_p = transposed(p)
    d, p, t_p = lax.optimization_barrier((d, p, t_p))
    t_d = transposed(d)
    cols_pair = start_around(p, ROW)
    t_d, cols_pair = lax.optimization_barrier((t_d, cols_pair))
    rows = spread(jnp.concatenate([t_p, t_d], 0), SIDE)
    cols_ends = ends_around(cols_pair, ROW)
    cols = columns(finish_around(cols_pair, *cols_ends, ROW))
    rows, *cols = lax.optimization_barrier((rows, *cols))
    others = swap(rows)
    gram_tile = (product(rows[:, :n], cols[0]) + product(others[:, :n], cols[1])) / tokens
    cross_tile = (product(rows[:, n:], cols[0]) + product(others[:, n:], cols[1])) / tokens
    return (gram_tile, cross_tile)


def solution(mesh):
    split = Mesh(mesh.devices.reshape(4, 2, 4, 2, 2), ROW + COL)
    in_specs = (P(COL, ROW), P(COL, ROW), P(ROW, COL), P(COL, ROW))
    out_specs = (P(ROW, COL), P(ROW, COL))
    return jax.shard_map(local, mesh=split, in_specs=in_specs, out_specs=out_specs, check_vma=False)
```

```python
import functools

import jax
import jax.numpy as jnp
from jax import lax
from jax.experimental import pallas as pl
from jax.experimental.pallas import tpu as pltpu
from jax.sharding import Mesh
from jax.sharding import PartitionSpec as P

ROW = ("x", "yl")
SIDE = ("z", "yh")
COL = ("z", "yh", "k")
BF = jnp.bfloat16
F32 = jnp.float32


PLACES = ((0, 0), (0, 1), (3, 0), (1, 0), (3, 1), (1, 1), (2, 0), (2, 1))


def step(a, dz, dy, axes=SIDE):
    nz, ny = lax.axis_size(axes[0]), lax.axis_size(axes[1])
    pairs = [
        (z * ny + y, ((z + dz) % nz) * ny + (y + dy) % ny) for z in range(nz) for y in range(ny)
    ]
    return lax.ppermute(a, axes, pairs)


def swap(a):
    return lax.ppermute(a, "k", [(0, 1), (1, 0)])


def after(a, *done):
    return lax.optimization_barrier((a,) + done)[0]


def transposed(a):
    pairs = []
    for r in range(8):
        for c in range(8):
            for k in range(2):
                pairs.append(((r * 8 + c) * 2 + k, (c * 8 + r) * 2 + k))
    return lax.ppermute(a, ROW + COL, pairs)


def spread(a, axes):
    n = lax.axis_size(axes)
    return lax.all_to_all(jnp.broadcast_to(a, (n,) + a.shape), axes, 0, 0, tiled=True)


def pruned(weight, words):
    n = weight.shape[1]
    rows = words.shape[0]
    halves = jnp.concatenate([words & 255, jnp.right_shift(words, 8)], 0).astype(BF)
    column = jnp.arange(n)
    source = column // 16 + rows * (column % 16 // 8)
    ones = (jnp.arange(2 * rows)[:, None] == source[None, :]).astype(BF)
    dims = (((0,), (0,)), ((), ()))
    byte = lax.dot_general(halves, ones, dims, preferred_element_type=F32).astype(jnp.int32)
    flag = jnp.right_shift(byte, (column % 8)[None, :]) & 1
    return jnp.where(flag == 1, weight, jnp.zeros_like(weight))


def dots(blocks, weights):
    a = jnp.concatenate(blocks, 0)
    outs = [jnp.dot(a, w, preferred_element_type=F32) for w in weights]
    return [o.reshape(len(blocks), -1, o.shape[1]) for o in outs]


def joined(first, second):
    return jnp.concatenate([jnp.concatenate(h, 2) for h in (first, second)], 0)


def arrange_kernel(at_ref, pair, up, down, across, side_across, out):
    n = across.shape[0]
    blocks = [pair[:n], pair[n:], up[:n], down[:n], up[n:], down[n:], across[...], side_across[...]]
    for i, b in enumerate(blocks):
        out[at_ref[i]] = b


def arranged(parts, at):
    vmem = pl.BlockSpec(memory_space=pltpu.VMEM)
    return pl.pallas_call(
        arrange_kernel,
        in_specs=[pl.BlockSpec(memory_space=pltpu.SMEM)] + [vmem] * 5,
        out_specs=vmem,
        out_shape=jax.ShapeDtypeStruct((8,) + parts[3].shape, BF),
        compiler_params=pltpu.CompilerParams(vmem_limit_bytes=4 * 1024 * 1024),
        name="arranged",
    )(jnp.stack(at).astype(jnp.int32), *parts)


def start_around(a, axes):
    return jnp.concatenate([a, step(a, 0, 1, axes)], 0)


def ends_around(pair, axes):
    return step(pair, 1, 0, axes), step(pair, 3, 0, axes)


def finish_around(pair, up, down, axes):
    n = pair.shape[0] // 2
    return pair, up, down, step(up[:n], 1, 0, axes), step(down[n:], 3, 0, axes)


def summed(sent, partial):
    own = lax.dynamic_index_in_dim(partial, lax.axis_index(ROW), 0, False)
    came = lax.all_to_all(sent, ROW, 0, 0, tiled=True)
    total = jnp.sum(came.astype(F32), 0) + (own - own.astype(BF).astype(F32))
    half = total.shape[1] // 2
    crossed = jnp.concatenate([total[:, half:], total[:, :half]], 1)
    return jnp.where(lax.axis_index("k") == 0, total, crossed).astype(BF)


def lookup(table, at):
    out = 0
    for i, t in enumerate(table):
        out = out + jnp.where(at == i, t, 0)
    return out


def columns(parts):
    x, yl, z, yh = (lax.axis_index(a) for a in ROW + SIDE)
    number = [PLACES.index((i // 2, i % 2)) for i in range(8)]
    at = []
    for a, b in PLACES:
        member = (x + a) % 4 * 2 + (yl + b) % 2
        far = [lookup([place[q] for place in PLACES], member) for q in range(2)]
        at.append(lookup(number, (z - x + far[0] + 4) % 4 * 2 + (yh - yl + far[1] + 2) % 2))
    every = arranged(parts, at)
    k = lax.axis_index("k")
    half = every.shape[2] // 2
    mine = lax.dynamic_slice_in_dim(every, k * half, half, 2)
    others = lax.dynamic_slice_in_dim(every, (1 - k) * half, half, 2)
    return mine, swap(others)


def product(rows, cols):
    dims = (((0, 1), (0, 1)), ((), ()))
    return lax.dot_general(rows, cols, dims, preferred_element_type=F32)


def local(dense_in, pruned_in, weight, keep_bits):
    tokens = dense_in.shape[0] * lax.axis_size(COL)
    n = dense_in.shape[0]
    h = n // 2
    p_side, p_up, p_down = step(pruned_in, 0, 1), step(pruned_in, 1, 0), step(pruned_in, 3, 0)
    weight_o = swap(weight)
    pruned_w = pruned(weight, keep_bits)
    p_side, p_up, p_down, pruned_w = lax.optimization_barrier((p_side, p_up, p_down, pruned_w))
    pruned_o = swap(pruned_w)
    p_up2 = step(jnp.concatenate([p_side, p_up[: n // 2]], 0), 1, 0)
    p_down2 = step(jnp.concatenate([p_side, p_down[n // 2 :]], 0), 3, 0)
    d_side = step(after(dense_in, p_side), 0, 1)
    p_up2, p_down2, d_side = lax.optimization_barrier((p_up2, p_down2, d_side))
    p_across = jnp.concatenate([p_up2[n:], p_down2[n:]], 0)
    p_side_across = step(p_across, 0, 1)
    d_pair = jnp.concatenate([dense_in, d_side], 0)
    d_up, d_down = step(d_pair, 1, 0), step(d_pair, 3, 0)
    pruned_ws, dense_ws = (pruned_w, pruned_o), (weight, weight_o)
    p_first = dots([pruned_in, p_side, p_up, p_down], pruned_ws)
    p_second = dots([p_up2[:n], p_down2[:n], p_across, p_side_across], pruned_ws)
    part_p = joined(p_first, p_second)
    sent_p = part_p.astype(BF)
    d_up, d_down, part_p, sent_p = lax.optimization_barrier((d_up, d_down, part_p, sent_p))
    p = summed(sent_p, part_p)
    d_across, d_side_across = step(d_up[:n], 1, 0), step(d_down[n:], 3, 0)
    d_first = dots([dense_in, d_side, d_up[:n], d_down[:n]], dense_ws)
    d_across, d_side_across, p, *d_first = lax.optimization_barrier((d_across, d_side_across, p, *d_first))
    d_second = dots([d_up[n:], d_down[n:], d_across, d_side_across], dense_ws)
    part_d = joined(d_first, d_second) - part_p
    sent_d = part_d.astype(BF)
    t_p = transposed(p)
    p, t_p, part_d, sent_d = lax.optimization_barrier((p, t_p, part_d, sent_d))
    d = summed(sent_d, part_d)
    d, p, t_p = lax.optimization_barrier((d, p, t_p))
    t_d = transposed(d)
    cols_pair = start_around(p, ROW)
    t_d, cols_pair = lax.optimization_barrier((t_d, cols_pair))
    rows = spread(jnp.concatenate([t_p, t_d], 0), SIDE)
    cols_ends = ends_around(cols_pair, ROW)
    cols = columns(finish_around(cols_pair, *cols_ends, ROW))
    rows, *cols = lax.optimization_barrier((rows, *cols))
    others = swap(rows)
    gram_tile = (product(rows[:, :n], cols[0]) + product(others[:, :n], cols[1])) / tokens
    cross_tile = (product(rows[:, n:], cols[0]) + product(others[:, n:], cols[1])) / tokens
    return (gram_tile, cross_tile)


def solution(mesh):
    split = Mesh(mesh.devices.reshape(4, 2, 4, 2, 2), ROW + COL)
    in_specs = (P(COL, ROW), P(COL, ROW), P(ROW, COL), P(COL, ROW))
    out_specs = (P(ROW, COL), P(ROW, COL))
    return jax.shard_map(local, mesh=split, in_specs=in_specs, out_specs=out_specs, check_vma=False)
```
